128 devices in a mesh: row: 8 (over x, core), col: 16 (over z, y).
Axes of the slice: x: 4, y: 4, z: 4, core: 2. Of those that a mesh axis runs over, the one named last changes fastest.
Arguments:
- vertex_panel: bfloat16 [32768, 512], P('row'), may hold values from -1.1953125 to 1.1953125
- context_panel: bfloat16 [8192, 512], P('col'), may hold values from -1.1953125 to 1.1953125
- hot_table: bfloat16 [1024, 512], replicated, may hold values from -1.1953125 to 1.1953125
- matching: int32 [2, 16], replicated, may hold values from 0 to 15, as said below
- hot_map: int32 [8, 16, 256], P('row', 'col'), may hold values from 0 to 1023
- cold_list: int32 [8, 16, 16, 64], P('row'), may hold values from 0 to 255
- cold_count: int32 [8, 16, 16], P('row'), may hold values from 17 to 64, as said below
- src_code: int32 [8, 16, 2, 128, 128], P('row', 'col'), may hold values from 0 to 1279, as said below
- ctx_rows: int32 [8, 16, 2, 128, 128], P('row', 'col'), may hold values from 0 to 511
- neg_tiles: int32 [8, 16, 2, 128], P('row', 'col'), may hold values from 0 to 3
Outputs:
- vertex_new: float32 [32768, 512], P(('row', 'col'))
- context_new: float32 [8192, 512], P('col')
- hot_new: float32 [1024, 512], replicated
The draws below stay inside these ranges and needn't reach their ends.
Inputs may be any that keep to these rules, and one draw needn't show every extreme that they name: In sub-episode s every partition c is paired with matching[s, c] = c xor m_s, with one number m_s of 1 to 15 common to all c. `cold_count`: in each vertex partition some owner receives exactly 64 live slots from every sender. `src_code`: A code below 256 names hot slot code; a code j + 256 names cold slot k = j % 64 of owner o = j // 64, and then k < cold_count[r, c, o].
All inputs are finite; a program needn't handle non-finite values.
Results may differ from the reference program's by a relative error of at most 0.0033.
Values may be sent and summed in bfloat16 or wider, within the bound.
No kernel may reach another device: no remote copies, remote signals or barrier semaphores. Data moves between devices by JAX's collectives and lax.ppermute only.
A program may use at most 128 MiB of HBM per device.

```python
import math
import jax
import jax.numpy as jnp
import numpy as np
from jax import lax

D = 512
BLOCK = 128
EPIS = 2
VS = 256
VERTICES = 32768
CR = 512
CONTEXTS = 8192
HOT = 1024
LHOT = 256
CAP = 64
NBLK = 128
N_ROW = 8
N_COL = 16


def count_table(key):
    key = jax.random.fold_in(key, 101)
    low_key, full_key = jax.random.split(key)
    base = jax.random.randint(low_key, (N_ROW, N_COL, N_COL), CAP // 4 + 1, CAP + 1)
    filled = jax.random.randint(full_key, (N_ROW, 1, 1), 0, N_COL)
    owners = jnp.arange(N_COL, dtype=jnp.int32).reshape(1, 1, N_COL)
    first_row = jnp.arange(N_ROW, dtype=jnp.int32).reshape(N_ROW, 1, 1) == 0
    base = jnp.where(owners == filled, CAP, base)
    base = jnp.where(first_row & (owners == N_COL - 1), CAP, base)
    return base.astype(jnp.int32)


def draw_cold_count(key, part):
    return count_table(key)


def draw_src_code(key, part):
    counts = count_table(key)
    key = jax.random.fold_in(key, 5)
    keys = jax.random.split(key, 5)
    shape = (N_ROW, N_COL, EPIS, NBLK, BLOCK)
    is_hot = jax.random.randint(keys[0], shape, 0, 4) == 0
    hot_code = jax.random.randint(keys[1], shape, 0, LHOT)
    owner = jax.random.randint(keys[2], shape, 0, N_COL)
    row_ids = jnp.arange(N_ROW, dtype=jnp.int32).reshape(N_ROW, 1, 1, 1, 1)
    col_ids = jnp.arange(N_COL, dtype=jnp.int32).reshape(1, N_COL, 1, 1, 1)
    limit = counts.reshape(-1)[(row_ids * N_COL + col_ids) * N_COL + owner]
    slot = jax.random.randint(keys[3], shape, 0, 1 << 20) % limit
    codes = jnp.where(is_hot, hot_code, LHOT + owner * CAP + slot)
    picks = jax.random.randint(keys[4], (3,), 0, 1 << 20)
    pick_col = picks[0] % N_COL
    pick_blk = picks[1] % NBLK
    pick_row = picks[2] % BLOCK
    blk_ids = jnp.arange(NBLK, dtype=jnp.int32).reshape(1, 1, 1, NBLK, 1)
    pos_ids = jnp.arange(BLOCK, dtype=jnp.int32).reshape(1, 1, 1, 1, BLOCK)
    epi_ids = jnp.arange(EPIS, dtype=jnp.int32).reshape(1, 1, EPIS, 1, 1)
    chosen = (row_ids == 0) & (col_ids == pick_col) & (epi_ids == 0) & (blk_ids == pick_blk) & (pos_ids == pick_row)
    codes = jnp.where(chosen, LHOT + N_COL * CAP - 1, codes)
    return codes.astype(jnp.int32)


def draw_matching(key, part):
    key = jax.random.fold_in(key, 7)
    offsets = jax.random.randint(key, (EPIS, 1), 1, N_COL)
    return jnp.bitwise_xor(jnp.arange(N_COL, dtype=jnp.int32)[None, :], offsets).astype(jnp.int32)


def place_ends(entries, own_key, least, high):
    spot = [jax.random.randint(jax.random.fold_in(own_key, axis), (), 0, length) for axis, length in enumerate(entries.shape)]
    widest = entries.shape.index(max(entries.shape))
    beside = spot[:widest] + [(spot[widest] + 1) % entries.shape[widest]] + spot[widest + 1:]
    return entries.at[tuple(spot)].set(least).at[tuple(beside)].set(high)


def shard_levels(rng, shape, shards, least, largest):
    gain, own = 1.0, jax.random.fold_in(rng, 6)
    for axis_at, shards_of in shards:
        steps = jnp.exp(jax.random.uniform(jax.random.fold_in(own, axis_at), (shards_of,), jnp.float32, least / len(shards), largest / len(shards)))
        gain = gain * jnp.repeat(steps, shape[axis_at] // shards_of).reshape([-1 if axis == axis_at else 1 for axis in range(len(shape))])
    return gain


def cumulative_ranks(count, slope):
    weights = [(1 << 20) // math.isqrt(standing ** slope) + 1 for standing in range(1, count + 1)]
    deviation = 1 + sum(weights) // (1 << 30)
    return np.cumsum(np.array([max(1, weight // deviation) for weight in weights]))


def skewed_ids(key, extent, number_of, slope):
    grid = cumulative_ranks(number_of, slope)
    ticket = jax.random.randint(jax.random.fold_in(key, 1), extent, 0, int(grid[number_of - 1]))
    grade = jnp.searchsorted(jnp.asarray(grid, jnp.int32), ticket, side="right")
    return jax.random.permutation(jax.random.fold_in(key, 2), number_of)[grade].astype(jnp.int32)


def noise(rng, extent, scale, most, cuts=(), held_as=jnp.bfloat16):
    result = scale * jax.random.normal(rng, extent, jnp.float32)
    if cuts:
        result = result * shard_levels(rng, extent, cuts, -0.22, 0.18)
    return jnp.clip(result, -most, most).astype(held_as)


def setup_inputs(seed: int = 0) -> dict:
    seeds = jax.random.split(jax.random.key(seed), 11)
    return {
        "vertex_panel": noise(seeds[0], (VERTICES, D), 0.2, 1.1953125, ((0, 8),)),
        "context_panel": noise(seeds[1], (CONTEXTS, D), 0.2, 1.1953125, ((0, 16),)),
        "hot_table": noise(seeds[2], (HOT, D), 0.2, 1.1953125),
        "matching": draw_matching(jax.random.fold_in(seeds[10], 71), 0),
        "hot_map": place_ends(skewed_ids(seeds[4], (N_ROW, N_COL, LHOT), HOT, 1), jax.random.fold_in(seeds[4], 3), 0, HOT - 1).astype(jnp.int32),
        "cold_list": place_ends(jax.random.randint(seeds[5], (N_ROW, N_COL, N_COL, CAP), 0, VS), jax.random.fold_in(seeds[5], 1), 0, VS - 1).astype(jnp.int32),
        "cold_count": draw_cold_count(jax.random.fold_in(seeds[10], 71), 0),
        "src_code": draw_src_code(jax.random.fold_in(seeds[10], 71), 0),
        "ctx_rows": place_ends(jax.random.randint(seeds[8], (N_ROW, N_COL, EPIS, NBLK, BLOCK), 0, CR), jax.random.fold_in(seeds[8], 1), 0, CR - 1).astype(jnp.int32),
        "neg_tiles": place_ends(jax.random.randint(seeds[9], (N_ROW, N_COL, EPIS, NBLK), 0, CR // BLOCK), jax.random.fold_in(seeds[9], 1), 0, (CR // BLOCK) - 1).astype(jnp.int32),
    }


NEG_WEIGHT = 0.0625
LEARN_RATE = 0.25


def episode_grads(slot_table, codes, row_ids, tile_ids, ctx_panel):
    width = slot_table.shape[1]
    block_rows = codes.shape[1]
    sources = slot_table[codes].astype(jnp.float32)
    positive = ctx_panel[row_ids].astype(jnp.float32)
    tile_view = ctx_panel.reshape(-1, block_rows, width)
    negative = tile_view[tile_ids].astype(jnp.float32)
    pos_score = jnp.einsum("nbd,nbd->nb", sources, positive)
    neg_score = jnp.einsum("nid,njd->nij", sources, negative)
    pos_grad = -jax.nn.sigmoid(-pos_score)
    neg_grad = lax.optimization_barrier((NEG_WEIGHT * jax.nn.sigmoid(neg_score)).astype(jnp.bfloat16)).astype(jnp.float32)
    source_grad = pos_grad[..., None] * positive + jnp.einsum("nij,njd->nid", neg_grad, negative)
    slot_grad = jnp.zeros(slot_table.shape, jnp.float32).at[codes.reshape(-1)].add(source_grad.reshape(-1, width))
    context_grad = jnp.zeros(ctx_panel.shape, jnp.float32).at[row_ids.reshape(-1)].add((pos_grad[..., None] * sources).reshape(-1, width))
    tile_grad = jnp.zeros(tile_view.shape, jnp.float32).at[tile_ids].add(jnp.einsum("nij,nid->njd", neg_grad, sources))
    return slot_grad, context_grad + tile_grad.reshape(-1, width)


def slot_rows(part_panel, hot_table, hot_list, own_lists, own_counts):
    col_count, capacity = own_lists.shape
    per_owner = part_panel.shape[0] // col_count
    cold_ids = (jnp.arange(col_count, dtype=jnp.int32)[:, None] * per_owner + own_lists).reshape(-1)
    in_list = (jnp.arange(capacity, dtype=jnp.int32)[None, :] < own_counts[:, None]).reshape(-1, 1)
    cold_emb = jnp.where(in_list, part_panel[cold_ids], jnp.zeros((), part_panel.dtype))
    return jnp.concatenate([hot_table[hot_list], cold_emb], 0), cold_ids, in_list


def reference(vertex_panel, context_panel, hot_table, matching, hot_map, cold_list, cold_count, src_code, ctx_rows, neg_tiles):
    part_rows = VS * N_COL

    def visit(totals, device):
        vertex_acc, context_acc, hot_acc = totals
        row_index = device // N_COL
        col_index = device % N_COL
        part_panel = lax.dynamic_slice_in_dim(vertex_panel, (row_index * part_rows).astype(jnp.int32), part_rows, 0)
        slot_table, cold_ids, in_list = slot_rows(part_panel, hot_table, hot_map[row_index, col_index], cold_list[row_index, col_index], cold_count[row_index, col_index])
        slot_total = jnp.zeros(slot_table.shape, jnp.float32)
        for episode in range(EPIS):
            partner = matching[episode, col_index]
            ctx_panel = lax.dynamic_slice_in_dim(context_panel, (partner * CR).astype(jnp.int32), CR, 0)
            slot_grad, context_grad = episode_grads(slot_table, src_code[row_index, col_index, episode], ctx_rows[row_index, col_index, episode], neg_tiles[row_index, col_index, episode], ctx_panel)
            slot_total = slot_total + slot_grad
            start = (jnp.int32(episode), (partner * CR).astype(jnp.int32), jnp.int32(0))
            current = lax.dynamic_slice(context_acc, start, (1, CR, D))
            context_acc = lax.dynamic_update_slice(context_acc, current + context_grad[None], start)
        hot_acc = hot_acc.at[hot_map[row_index, col_index]].add(slot_total[:LHOT])
        cold_grad = jnp.where(in_list, slot_total[LHOT:], 0.0)
        vertex_acc = vertex_acc.at[(row_index * part_rows + cold_ids).astype(jnp.int32)].add(cold_grad)
        return (vertex_acc, context_acc, hot_acc), None

    start_totals = (jnp.zeros(vertex_panel.shape, jnp.float32), jnp.zeros((EPIS,) + context_panel.shape, jnp.float32), jnp.zeros(hot_table.shape, jnp.float32))
    totals, unused = lax.scan(visit, start_totals, jnp.arange(N_ROW * N_COL, dtype=jnp.int32))
    vertex_acc, context_acc, hot_acc = totals
    context_step = lax.optimization_barrier(context_acc.astype(jnp.bfloat16)).astype(jnp.float32)
    vertex_new = vertex_panel.astype(jnp.float32) - LEARN_RATE * vertex_acc
    context_new = context_panel.astype(jnp.float32) - LEARN_RATE * jnp.sum(context_step, 0)
    hot_new = hot_table.astype(jnp.float32) - LEARN_RATE * hot_acc
    return (vertex_new, context_new, hot_new)
```

```python
import functools

import jax
import jax.numpy as jnp
import numpy as np
from jax import lax
from jax.experimental import pallas as pl
from jax.experimental.pallas import tpu as pltpu
from jax.sharding import Mesh, PartitionSpec as P

NEG_WEIGHT = 0.0625
LEARN_RATE = 0.25

D = 512
BLOCK = 128
HOT = 1024
LHOT = 256
CAP = 64
VS = 256
CR = 512
NX = 4
NCORE = 2
NCOL = 16
NBLK = 128
SLOTS = LHOT + NCOL * CAP
HALF_SLOTS = SLOTS // 2
CHUNK = 16
BASE = 4096.0

F32 = jnp.float32
BF16 = jnp.bfloat16
I16 = jnp.int16
NN = (((1,), (0,)), ((), ()))
NT = (((1,), (1,)), ((), ()))
TN = (((0,), (0,)), ((), ()))


def dot(a, b, dims):
    return lax.dot_general(a, b, dims, preferred_element_type=F32)


def params(mib):
    return pltpu.CompilerParams(vmem_limit_bytes=mib * 2**20)


def cost(flops, nbytes):
    return pl.CostEstimate(flops=flops, bytes_accessed=nbytes, transcendentals=0)


def one_hot(rows, ids, weight=None):
    shape = (rows, ids.shape[1])
    index = lax.broadcasted_iota(jnp.int32, shape, 0).astype(I16)
    hit = index == jnp.broadcast_to(ids.astype(I16), shape)
    value = jnp.ones((), BF16) if weight is None else jnp.broadcast_to(weight, shape)
    return jnp.where(hit, value, jnp.zeros((), BF16))


def split(x):
    high = x.astype(BF16)
    return high, (x - high.astype(F32)).astype(BF16)


def count_kernel(episode, tiles, codes, rows, pairs, tile_counts, left, right, left2, right2):
    step = pl.program_id(0)

    @pl.when(step == 0)
    def _():
        pairs[...] = jnp.zeros_like(pairs)
        tile_counts[...] = jnp.zeros_like(tile_counts)

    for n in range(CHUNK):
        at = slice(n * BLOCK, (n + 1) * BLOCK)
        code = codes[n : n + 1, :]
        upper = code >= HALF_SLOTS
        weight = jnp.where(upper, BASE, 1.0).astype(BF16)
        left[:, at] = one_hot(HALF_SLOTS, jnp.where(upper, code - HALF_SLOTS, code), weight)
        right[:, at] = one_hot(CR, rows[n : n + 1, :])
        tile = tiles[episode * NBLK + step * CHUNK + n]
        left2[:, at] = one_hot(48, code >> 5)
        right2[:, at] = one_hot(128, (code & 31) * 4 + tile)
    packed = dot(left[...], right[...], NT)
    high = jnp.floor(packed * (1.0 / BASE))
    pairs[0:HALF_SLOTS] += packed - high * BASE
    pairs[HALF_SLOTS:SLOTS] += high
    tile_counts[...] += dot(left2[...], right2[...], NT)


def edge_counts(episode, src_code, ctx_rows, neg_tiles):
    block = pl.BlockSpec((None, None, None, CHUNK, BLOCK), lambda i, t: (0, 0, episode, i, 0))
    width = CHUNK * BLOCK
    return pl.pallas_call(
        functools.partial(count_kernel, episode),
        out_shape=[
            jax.ShapeDtypeStruct((SLOTS, CR), F32),
            jax.ShapeDtypeStruct((48, 128), F32),
        ],
        grid_spec=pltpu.PrefetchScalarGridSpec(
            num_scalar_prefetch=1,
            grid=(NBLK // CHUNK,),
            in_specs=[block, block],
            out_specs=[
                pl.BlockSpec((SLOTS, CR), lambda i, t: (0, 0)),
                pl.BlockSpec((48, 128), lambda i, t: (0, 0)),
            ],
            scratch_shapes=[
                pltpu.VMEM((HALF_SLOTS, width), BF16),
                pltpu.VMEM((CR, width), BF16),
                pltpu.VMEM((48, width), BF16),
                pltpu.VMEM((128, width), BF16),
            ],
        ),
        compiler_params=params(40),
        cost_estimate=cost(2 * NBLK * BLOCK * HALF_SLOTS * CR, 3 << 20),
        name="edge_counts",
    )(neg_tiles.reshape(-1), src_code, ctx_rows)


def slot_kernel(panel, hot_table, hot_list, cold_ids, out):
    owners = pl.program_id(0)

    @pl.when(owners == 0)
    def _():
        out[...] = dot(one_hot(HOT, hot_list[...]), hot_table[...], TN).astype(BF16)

    @pl.when(owners > 0)
    def _():
        for o in range(4):
            ids = cold_ids[o : o + 1, :]
            rows = dot(one_hot(VS, ids), panel[o * VS : (o + 1) * VS, :], TN)
            out[o * CAP : (o + 1) * CAP, :] = rows.astype(BF16)


def slot_rows(panel, hot_table, hot_list, cold_ids):
    later = lambda i: (jnp.maximum(i - 1, 0), 0)
    return pl.pallas_call(
        slot_kernel,
        out_shape=jax.ShapeDtypeStruct((SLOTS, D), BF16),
        grid=(5,),
        in_specs=[
            pl.BlockSpec((4 * VS, D), later),
            pl.BlockSpec((HOT, D), lambda i: (0, 0)),
            pl.BlockSpec((1, LHOT), lambda i: (0, 0)),
            pl.BlockSpec((None, 4, CAP), lambda i: (jnp.maximum(i - 1, 0), 0, 0)),
        ],
        out_specs=pl.BlockSpec((LHOT, D), lambda i: (i, 0)),
        compiler_params=params(24),
        cost_estimate=cost(1 << 29, 6 << 20),
        name="slot_rows",
    )(panel, hot_table, hot_list, cold_ids.reshape(4, 4, CAP))


def pick_kernel(matching, pieces, out):
    for episode in range(2):
        for reader in range(NCOL):
            partner = matching[episode * NCOL + reader]
            out[reader, episode] = pieces[partner]


def pick_pieces(matching, pieces):
    rows = pieces.shape[1]
    return pl.pallas_call(
        pick_kernel,
        out_shape=jax.ShapeDtypeStruct((NCOL, 2, rows, D), BF16),
        in_specs=[
            pl.BlockSpec(memory_space=pltpu.SMEM),
            pl.BlockSpec(memory_space=pltpu.VMEM),
        ],
        out_specs=pl.BlockSpec(memory_space=pltpu.VMEM),
        compiler_params=params(16),
        cost_estimate=cost(0, 2 << 20),
        name="pick_pieces",
    )(matching.reshape(-1), pieces)


def grad_kernel(
    core, slots, ctx, pairs0, pairs1, counts0, counts1, hot_list, cold, keep, send, ctx_acc, hot_acc
):
    step = pl.program_id(0)

    @pl.when(step == 0)
    def _():
        ctx_acc[...] = jnp.zeros_like(ctx_acc)

    here = slots[...]
    slot_at = step * LHOT + lax.broadcasted_iota(jnp.int32, (LHOT, 48), 0)
    group = ((slot_at >> 5) == lax.broadcasted_iota(jnp.int32, (LHOT, 48), 1)).astype(F32).astype(BF16)
    lane = lax.broadcasted_iota(jnp.int32, (LHOT, 256), 1)
    slot_in = lax.broadcasted_iota(jnp.int32, (LHOT, 256), 0) & 31
    mine = ((lane & 127) >> 2) == slot_in
    pick_row = lax.broadcasted_iota(jnp.int32, (256, CR), 0)
    pick_col = lax.broadcasted_iota(jnp.int32, (256, CR), 1)
    spread = jnp.where(
        (pick_row & 3) == (pick_col >> 7), jnp.where(pick_row >= 128, 128.0, 1.0), 0.0
    ).astype(BF16)
    slot_grad = jnp.zeros((LHOT, D), F32)
    for episode in range(2):
        panel = ctx[:, episode].reshape(CR, D)
        counted = (pairs0, pairs1)[episode][...]
        table = (counts0, counts1)[episode][...]
        upper = jnp.floor(table * (1.0 / 128.0))
        both = jnp.concatenate([table - upper * 128.0, upper], 1).astype(BF16)
        taken = jnp.where(mine, dot(group, both, NN), 0.0).astype(BF16)
        tiled = dot(taken, spread, NN)
        score = dot(here, panel, NT)
        curve = jnp.tanh(0.5 * score)
        negative = (0.5 * NEG_WEIGHT + (0.5 * NEG_WEIGHT) * curve).astype(BF16).astype(F32)
        grad = tiled * negative - counted * (0.5 - 0.5 * curve)
        high, low = split(grad)
        slot_grad += dot(high, panel, NN) + dot(low, panel, NN)
        ctx_acc[episode] += dot(high, here, TN) + dot(low, here, TN)

    @pl.when(step == 0)
    def _():
        high, low = split(slot_grad)
        where_hot = one_hot(HOT, hot_list[...])
        hot_acc[...] = dot(where_hot, high, NN) + dot(where_hot, low, NN)

    @pl.when(step > 0)
    def _():
        cold[...] = slot_grad.astype(BF16)

    @pl.when(step == pl.num_programs(0) - 1)
    def _():
        for half, out in ((core[0], keep), (1 - core[0], send)):
            for x in range(NX):
                hot_at = pl.multiple_of(half * (HOT // 2) + x * 128, 128)
                ctx_at = pl.multiple_of(half * (CR // 2) + x * 64, 64)
                out[x, 0:128] = hot_acc[pl.ds(hot_at, 128)]
                out[x, 128:192] = ctx_acc[0, pl.ds(ctx_at, 64)]
                out[x, 192:256] = ctx_acc[1, pl.ds(ctx_at, 64)]


def gradients(core, slots, ctx, counts, hot_list):
    (pairs0, tiles0), (pairs1, tiles1) = counts
    chunk = pl.BlockSpec((LHOT, CR), lambda i, c: (i, 0))
    whole = lambda *shape: pl.BlockSpec(shape, lambda i, c: (0,) * len(shape))
    part = jax.ShapeDtypeStruct((NX, 256, D), F32)
    return pl.pallas_call(
        grad_kernel,
        out_shape=[jax.ShapeDtypeStruct((NCOL * CAP, D), BF16), part, part],
        grid_spec=pltpu.PrefetchScalarGridSpec(
            num_scalar_prefetch=1,
            grid=(5,),
            in_specs=[
                chunk,
                whole(NCOL, 2, CR // NCOL, D),
                chunk,
                chunk,
                whole(48, 128),
                whole(48, 128),
                whole(1, LHOT),
            ],
            out_specs=[
                pl.BlockSpec((LHOT, D), lambda i, c: (jnp.maximum(i - 1, 0), 0)),
                whole(NX, 256, D),
                whole(NX, 256, D),
            ],
            scratch_shapes=[pltpu.VMEM((2, CR, D), F32), pltpu.VMEM((HOT, D), F32)],
        ),
        compiler_params=params(48),
        cost_estimate=cost(6 << 30, 12 << 20),
        name="gradients",
    )(core, slots, ctx, pairs0, pairs1, tiles0, tiles1, hot_list)


def x_sum_kernel(parts, out):
    total = parts[0].astype(F32)
    for x in range(1, NX):
        total += parts[x].astype(F32)
    for j in range(NCOL):
        pair = jnp.concatenate([total[j * 8 : j * 8 + 8], total[128 + j * 8 : 136 + j * 8]], 0)
        out[j] = pair.astype(BF16)


def x_sum(parts):
    return pl.pallas_call(
        x_sum_kernel,
        out_shape=jax.ShapeDtypeStruct((NCOL, 16, D), BF16),
        compiler_params=params(16),
        cost_estimate=cost(1 << 20, 2 << 20),
        name="x_sum",
    )(parts)


def col_sum_kernel(partner, parts, out):
    hot = parts[0].astype(F32)[0:8]
    for c in range(1, NCOL):
        hot += parts[c].astype(F32)[0:8]
    for q in range(NCOL):
        step = parts[partner[q]].astype(F32)[8:16]
        pair = jnp.concatenate([hot, step], 0).astype(BF16)
        for x in range(NX):
            out[x, q] = pair


def col_sum(partner, parts):
    return pl.pallas_call(
        col_sum_kernel,
        out_shape=jax.ShapeDtypeStruct((NX, NCOL, 16, D), BF16),
        in_specs=[
            pl.BlockSpec(memory_space=pltpu.SMEM),
            pl.BlockSpec(memory_space=pltpu.VMEM),
        ],
        out_specs=pl.BlockSpec(memory_space=pltpu.VMEM),
        compiler_params=params(16),
        cost_estimate=cost(1 << 20, 2 << 20),
        name="col_sum",
    )(partner, parts)


def finish_kernel(core, own, other, hot_table, context, hot_out, context_out):
    for from_other, parts in ((0, own), (1, other)):
        half = core[0] if from_other == 0 else 1 - core[0]
        for x in range(NX):
            hot_at = pl.multiple_of(half * (HOT // 2) + x * 128, 128)
            ctx_at = pl.multiple_of(half * (CR // 2) + x * 64, 64)
            first = [parts[x, j].astype(F32) for j in range(NCOL)]
            hot = jnp.concatenate([p[0:8] for p in first], 0)
            step = jnp.concatenate([first[j][8:16] + first[j + 8][8:16] for j in range(8)], 0)
            hot_rows = hot_table[pl.ds(hot_at, 128)].astype(F32)
            hot_out[pl.ds(hot_at, 128)] = hot_rows - LEARN_RATE * hot
            ctx_rows = context[pl.ds(ctx_at, 64)].astype(F32)
            context_out[pl.ds(ctx_at, 64)] = ctx_rows - LEARN_RATE * step


def finish(core, own, other, hot_table, context):
    vmem = pl.BlockSpec(memory_space=pltpu.VMEM)
    return pl.pallas_call(
        finish_kernel,
        out_shape=[jax.ShapeDtypeStruct((HOT, D), F32), jax.ShapeDtypeStruct((CR, D), F32)],
        in_specs=[pl.BlockSpec(memory_space=pltpu.SMEM), vmem, vmem, vmem, vmem],
        out_specs=[vmem, vmem],
        compiler_params=params(24),
        cost_estimate=cost(1 << 20, 7 << 20),
        name="finish",
    )(core, own, other, hot_table, context)


def vertex_kernel(col, ids, received, panel, out):
    total = jnp.zeros((VS, D), F32)
    for n in range(8):
        where_row = one_hot(VS, ids[n : n + 1, :])
        total += dot(where_row, received[n * 128 : (n + 1) * 128, :], NN)
    out[...] = panel[...].astype(F32) - LEARN_RATE * total


def vertex_rows(col, ids, received, panel):
    return pl.pallas_call(
        vertex_kernel,
        out_shape=jax.ShapeDtypeStruct((VS, D), F32),
        grid_spec=pltpu.PrefetchScalarGridSpec(
            num_scalar_prefetch=1,
            grid=(1,),
            in_specs=[
                pl.BlockSpec((8, 128), lambda i, c: (0, 0)),
                pl.BlockSpec((NCOL * CAP, D), lambda i, c: (0, 0)),
                pl.BlockSpec((VS, D), lambda i, c: (c[0], 0)),
            ],
            out_specs=pl.BlockSpec((VS, D), lambda i, c: (0, 0)),
        ),
        compiler_params=params(16),
        cost_estimate=cost(1 << 28, 2 << 20),
        name="vertex_rows",
    )(col, ids, received, panel)


def all_to_all(x, axes):
    return lax.all_to_all(x, axes, 0, 0, tiled=True)


def body(
    vertex_panel,
    context_panel,
    hot_table,
    matching,
    hot_map,
    cold_list,
    cold_count,
    src_code,
    ctx_rows,
    neg_tiles,
):
    col_index = lax.axis_index("col")
    core = lax.axis_index("core").astype(jnp.int32)[None]
    col = col_index.astype(jnp.int32)[None]
    hot_list = hot_map[0]
    live = jnp.arange(CAP, dtype=jnp.int32) < cold_count[0][..., None]
    ids = jnp.where(live, cold_list[0], -1)
    own_ids = lax.dynamic_index_in_dim(ids, col_index, 0, keepdims=False)
    sender_ids = lax.dynamic_index_in_dim(ids, col_index, 1, keepdims=False).reshape(8, 128)

    pieces = all_to_all(context_panel.reshape(NCOL, CR // NCOL, D), "col")
    counts = [edge_counts(0, src_code, ctx_rows, neg_tiles)]
    ctx = all_to_all(pick_pieces(matching, pieces), "col")
    counts.append(edge_counts(1, src_code, ctx_rows, neg_tiles))
    slots = slot_rows(vertex_panel, hot_table, hot_list, own_ids)

    cold, keep, send = gradients(core, slots, ctx, counts, hot_list)
    arrived = lax.ppermute(send, "core", [(0, 1), (1, 0)])
    received = all_to_all(cold.reshape(NCOL, CAP, D), "col").reshape(NCOL * CAP, D)
    parts = all_to_all((keep + arrived).astype(BF16), "x")
    parts = all_to_all(x_sum(parts), "col")
    episode = (col_index >= NCOL // 2).astype(jnp.int32)
    partner = lax.dynamic_index_in_dim(matching, episode, 0, keepdims=False)
    parts = col_sum(partner, parts).reshape(NX * NCOL, 16, D)
    own = all_to_all(parts, ("x", "col")).reshape(NX, NCOL, 16, D)
    other = lax.ppermute(own, "core", [(0, 1), (1, 0)])
    hot_new, context_new = finish(core, own, other, hot_table, context_panel)
    vertex_new = vertex_rows(col, sender_ids, received, vertex_panel)
    return (vertex_new, context_new, hot_new)


def solution(mesh):
    split_mesh = Mesh(mesh.devices.reshape(NX, NCORE, NCOL), ("x", "core", "col"))
    row = ("x", "core")
    in_specs = (
        P(row, None),
        P("col", None),
        P(),
        P(),
        P(row, "col", None),
        P(row, None, None, None),
        P(row, None, None),
        P(row, "col", None, None, None),
        P(row, "col", None, None, None),
        P(row, "col", None, None),
    )
    out_specs = (P(("x", "core", "col"), None), P("col", None), P())
    return jax.shard_map(
        body, mesh=split_mesh, in_specs=in_specs, out_specs=out_specs, check_vma=False
    )
```

```python
import functools

import jax
import jax.numpy as jnp
import numpy as np
from jax import lax
from jax.experimental import pallas as pl
from jax.experimental.pallas import tpu as pltpu
from jax.sharding import Mesh, PartitionSpec as P

NEG_WEIGHT = 0.0625
LEARN_RATE = 0.25

D = 512
BLOCK = 128
HOT = 1024
LHOT = 256
CAP = 64
VS = 256
CR = 512
NX = 4
NCORE = 2
NCOL = 16
NBLK = 128
SLOTS = LHOT + NCOL * CAP
HALF_SLOTS = SLOTS // 2
CHUNK = 16
STEPS = NBLK // CHUNK
BASE = 4096.0

F32 = jnp.float32
BF16 = jnp.bfloat16
I16 = jnp.int16
F8 = jnp.float8_e5m2
NN = (((1,), (0,)), ((), ()))
NT = (((1,), (1,)), ((), ()))
TN = (((0,), (0,)), ((), ()))


def dot(a, b, dims):
    return lax.dot_general(a, b, dims, preferred_element_type=F32)


def params(mib):
    return pltpu.CompilerParams(vmem_limit_bytes=mib * 2**20)


def cost(flops, nbytes):
    return pl.CostEstimate(flops=flops, bytes_accessed=nbytes, transcendentals=0)


def one_hot(rows, ids, weight=None):
    shape = (rows, ids.shape[1])
    index = lax.broadcasted_iota(jnp.int32, shape, 0).astype(I16)
    hit = index == jnp.broadcast_to(ids.astype(I16), shape)
    value = jnp.ones((), BF16) if weight is None else jnp.broadcast_to(weight, shape)
    return jnp.where(hit, value, jnp.zeros((), BF16))


def split(x):
    high = x.astype(BF16)
    return high, (x - high.astype(F32)).astype(BF16)


def count_step(first_row, pairs, codes, rows, left, right):
    width = right.shape[0]
    for n in range(CHUNK):
        at = slice(n * BLOCK, (n + 1) * BLOCK)
        code = codes[n : n + 1, :]
        upper = code >= HALF_SLOTS
        weight = jnp.where(upper, BASE, 1.0).astype(BF16)
        left[:, at] = one_hot(HALF_SLOTS, jnp.where(upper, code - HALF_SLOTS, code), weight)
        right[:, at] = one_hot(width, rows[n : n + 1, :] - first_row)
    packed = dot(left[...], right[...], NT)
    high = jnp.floor(packed * (1.0 / BASE))
    pairs[0:HALF_SLOTS] += packed - high * BASE
    pairs[HALF_SLOTS:SLOTS] += high


def tile_step(episode, step, tiles, tile_counts, codes, left, right):
    for n in range(CHUNK):
        at = slice(n * BLOCK, (n + 1) * BLOCK)
        code = codes[n : n + 1, :]
        tile = tiles[0, 0, episode, step * CHUNK + n]
        left[:, at] = one_hot(64, code >> 5).astype(F8)
        right[:, at] = one_hot(128, (code & 31) * 4 + tile).astype(F8)
    tile_counts[...] += dot(left[...], right[...], NT)


def first_count_kernel(codes, rows, pairs, left, right):
    @pl.when(pl.program_id(0) == 0)
    def _():
        pairs[...] = jnp.zeros_like(pairs)

    count_step(0, pairs, codes, rows, left, right)


def second_count_kernel(
    tiles, codes0, rows0, codes1, rows1, pairs0, tile_counts, pairs1,
    left0, right0, left1, right1, left2, right2,
):
    step = pl.program_id(0)

    @pl.when(step == 0)
    def _():
        pairs0[...] = jnp.zeros_like(pairs0)
        pairs1[...] = jnp.zeros_like(pairs1)
        tile_counts[...] = jnp.zeros_like(tile_counts)

    count_step(CR // 2, pairs0, codes0, rows0, left0, right0)
    count_step(0, pairs1, codes1, rows1, left1, right1)
    tile_step(0, step, tiles, tile_counts, codes0, left2, right2)


def count_scratch():
    edges = CHUNK * BLOCK
    return [pltpu.VMEM((HALF_SLOTS, edges), BF16), pltpu.VMEM((CR // 2, edges), BF16)]


def tile_scratch():
    edges = CHUNK * BLOCK
    return [pltpu.VMEM((64, edges), F8), pltpu.VMEM((128, edges), F8)]


SMEM = pl.BlockSpec(memory_space=pltpu.SMEM)


def whole(*shape):
    return pl.BlockSpec(shape, lambda i: (0,) * len(shape))


def edge_block(episode):
    return pl.BlockSpec(
        (None, None, None, CHUNK, BLOCK),
        lambda i: (0, 0, episode, jnp.minimum(i, STEPS - 1), 0),
    )


def first_counts(src_code, ctx_rows):
    return pl.pallas_call(
        first_count_kernel,
        out_shape=jax.ShapeDtypeStruct((SLOTS, CR // 2), F32),
        grid=(STEPS,),
        in_specs=[edge_block(0), edge_block(0)],
        out_specs=whole(SLOTS, CR // 2),
        scratch_shapes=count_scratch(),
        compiler_params=params(56),
        cost_estimate=cost(NBLK * BLOCK * HALF_SLOTS * CR, 3 << 20),
        name="first_counts",
    )(src_code, ctx_rows)


def second_counts(neg_tiles, src_code, ctx_rows):
    part = jax.ShapeDtypeStruct((SLOTS, CR // 2), F32)
    return pl.pallas_call(
        second_count_kernel,
        out_shape=[part, jax.ShapeDtypeStruct((64, 128), F32), part],
        grid=(STEPS,),
        in_specs=[SMEM, edge_block(0), edge_block(0), edge_block(1), edge_block(1)],
        out_specs=[whole(SLOTS, CR // 2), whole(64, 128), whole(SLOTS, CR // 2)],
        scratch_shapes=count_scratch() + count_scratch() + tile_scratch(),
        compiler_params=params(56),
        cost_estimate=cost(2 * NBLK * BLOCK * HALF_SLOTS * CR, 6 << 20),
        name="second_counts",
    )(neg_tiles, src_code, ctx_rows, src_code, ctx_rows)


def live_ids(ids, count):
    lane = lax.broadcasted_iota(jnp.int32, ids.shape, 1)
    return jnp.where(lane < count, ids, -1)


def pick_kernel(matching, pieces, out):
    for episode in range(2):
        for reader in range(NCOL):
            partner = matching[episode, reader]
            out[reader, episode] = pieces[partner]


def pick_pieces(matching, pieces):
    rows = pieces.shape[1]
    return pl.pallas_call(
        pick_kernel,
        out_shape=jax.ShapeDtypeStruct((NCOL, 2, rows, D), BF16),
        in_specs=[
            pl.BlockSpec(memory_space=pltpu.SMEM),
            pl.BlockSpec(memory_space=pltpu.VMEM),
        ],
        out_specs=pl.BlockSpec(memory_space=pltpu.VMEM),
        compiler_params=params(16),
        cost_estimate=cost(0, 2 << 20),
        name="pick_pieces",
    )(matching, pieces)


def main_kernel(
    tiles, cold_count, codes, rows, panel, hot_table, hot_list, cold_list, ctx,
    pairs0_low, pairs0_high, counts0, pairs1_low, cold, keep, send,
    left, right, left2, right2, pairs1_high, counts1, all_slots, all_grads, ctx_acc, hot_acc,
):
    step = pl.program_id(0)
    col = lax.axis_index("col")

    @pl.when(step == 0)
    def _():
        pairs1_high[...] = jnp.zeros_like(pairs1_high)
        counts1[...] = jnp.zeros_like(counts1)
        all_slots[0:LHOT] = dot(one_hot(HOT, hot_list[...]), hot_table[...], TN).astype(BF16)

    @pl.when(step < STEPS)
    def _():
        for o in range(2):
            owner = 2 * step + o
            ids = live_ids(cold_list[0, col, pl.ds(owner, 1), :], cold_count[0, col, owner])
            taken = dot(one_hot(VS, ids), panel[o * VS : (o + 1) * VS, :], TN)
            at = pl.multiple_of(LHOT + owner * CAP, CAP)
            all_slots[pl.ds(at, CAP)] = taken.astype(BF16)
        count_step(CR // 2, pairs1_high, codes, rows, left, right)
        tile_step(1, step, tiles, counts1, codes, left2, right2)

    @pl.when(step >= STEPS)
    def _():
        grad_step(
            step - STEPS, hot_list, ctx, pairs0_low, pairs0_high, counts0, pairs1_low, cold, keep,
            send, pairs1_high, counts1, all_slots, all_grads, ctx_acc, hot_acc,
        )


def grad_step(
    step, hot_list, ctx, pairs0_low, pairs0_high, counts0, pairs1_low, cold, keep, send,
    pairs1_high, counts1, all_slots, all_grads, ctx_acc, hot_acc,
):
    slot_rows = pl.ds(pl.multiple_of(step * LHOT, LHOT), LHOT)
    here = all_slots[slot_rows]
    slot_at = step * LHOT + lax.broadcasted_iota(jnp.int32, (LHOT, 64), 0)
    group = ((slot_at >> 5) == lax.broadcasted_iota(jnp.int32, (LHOT, 64), 1)).astype(F32).astype(BF16)
    lane = lax.broadcasted_iota(jnp.int32, (LHOT, 256), 1)
    slot_in = lax.broadcasted_iota(jnp.int32, (LHOT, 256), 0) & 31
    mine = ((lane & 127) >> 2) == slot_in
    pick_row = lax.broadcasted_iota(jnp.int32, (256, CR), 0)
    pick_col = lax.broadcasted_iota(jnp.int32, (256, CR), 1)
    spread = jnp.where(
        (pick_row & 3) == (pick_col >> 7), jnp.where(pick_row >= 128, 128.0, 1.0), 0.0
    ).astype(BF16)
    total = None
    grads = []
    for episode in range(2):
        panel = ctx[:, episode].reshape(CR, D)
        if episode == 0:
            counted = jnp.concatenate([pairs0_low[...], pairs0_high[...]], 1)
        else:
            counted = jnp.concatenate([pairs1_low[...], pairs1_high[slot_rows]], 1)
        table = (counts0, counts1)[episode][...]
        upper = jnp.floor(table * (1.0 / 128.0))
        both = jnp.concatenate([table - upper * 128.0, upper], 1).astype(BF16)
        taken = jnp.where(mine, dot(group, both, NN), 0.0).astype(BF16)
        tiled = dot(taken, spread, NN)
        curve = jnp.tanh(0.5 * dot(here, panel, NT))
        negative = (0.5 * NEG_WEIGHT + (0.5 * NEG_WEIGHT) * curve).astype(BF16).astype(F32)
        grad = tiled * negative - counted * (0.5 - 0.5 * curve)
        high = grad.astype(BF16)
        grads.append((grad, high, panel))
        part = dot(high, panel, NN)
        total = part if total is None else total + part
        all_grads[episode, slot_rows] = high

    @pl.when(step == 0)
    def _():
        full = total
        for grad, high, panel in grads:
            full = full + dot((grad - high.astype(F32)).astype(BF16), panel, NN)
        upper, lower = split(full)
        where_hot = one_hot(HOT, hot_list[...])
        hot_acc[...] = dot(where_hot, upper, NN) + dot(where_hot, lower, NN)

    @pl.when(step > 0)
    def _():
        for o in range(4):
            cold[o] = total[o * CAP : (o + 1) * CAP].astype(BF16)

    @pl.when(step == 4)
    def _():
        for episode in range(2):
            ctx_acc[episode] = dot(all_grads[episode], all_slots[...], TN)
        core = lax.axis_index("core")
        for half, out in ((core, keep), (1 - core, send)):
            for away in range(NX):
                x = lax.axis_index("x") ^ away
                hot_at = pl.multiple_of(half * (HOT // 2) + x * 128, 128)
                ctx_at = pl.multiple_of(half * (CR // 2) + x * 64, 64)
                out[away, 0:128] = hot_acc[pl.ds(hot_at, 128)].astype(out.dtype)
                out[away, 128:192] = ctx_acc[0, pl.ds(ctx_at, 64)].astype(out.dtype)
                out[away, 192:256] = ctx_acc[1, pl.ds(ctx_at, 64)].astype(out.dtype)


def gradients(
    neg_tiles, cold_count, src_code, ctx_rows, panel, hot_table, hot_list, cold_list, ctx, counts
):
    later = lambda i: jnp.maximum(i - STEPS, 0)
    half = pl.BlockSpec((LHOT, CR // 2), lambda i: (later(i), 0))
    part = lambda dtype: jax.ShapeDtypeStruct((NX, 256, D), dtype)
    return pl.pallas_call(
        main_kernel,
        out_shape=[jax.ShapeDtypeStruct((NCOL, CAP, D), BF16), part(F32), part(BF16)],
        grid=(STEPS + 5,),
        in_specs=[
            SMEM,
            SMEM,
            edge_block(1),
            edge_block(1),
            pl.BlockSpec((2 * VS, D), lambda i: (jnp.minimum(i, STEPS - 1), 0)),
            whole(HOT, D),
            whole(1, LHOT),
            whole(1, NCOL, NCOL, CAP),
            whole(NCOL, 2, CR // NCOL, D),
            half,
            half,
            whole(64, 128),
            half,
        ],
        out_specs=[
            pl.BlockSpec((4, CAP, D), lambda i: (later(i - 1), 0, 0)),
            whole(NX, 256, D),
            whole(NX, 256, D),
        ],
        scratch_shapes=count_scratch()
        + tile_scratch()
        + [
            pltpu.VMEM((SLOTS, CR // 2), F32),
            pltpu.VMEM((64, 128), F32),
            pltpu.VMEM((SLOTS, D), BF16),
            pltpu.VMEM((2, SLOTS, CR), BF16),
            pltpu.VMEM((2, CR, D), F32),
            pltpu.VMEM((HOT, D), F32),
        ],
        compiler_params=params(56),
        cost_estimate=cost(28 << 30, 12 << 20),
        name="gradients",
    )(
        neg_tiles, cold_count, src_code, ctx_rows, panel, hot_table, hot_list, cold_list, ctx,
        *counts,
    )


def x_sum_kernel(own, first, second, third, out):
    total = own[...]
    for part in (first, second, third):
        total += part[...].astype(F32)
    for j in range(NCOL):
        pair = jnp.concatenate([total[j * 8 : j * 8 + 8], total[128 + j * 8 : 136 + j * 8]], 0)
        out[j] = pair.astype(BF16)


def x_sum(own, others):
    return pl.pallas_call(
        x_sum_kernel,
        out_shape=jax.ShapeDtypeStruct((NCOL, 16, D), BF16),
        compiler_params=params(16),
        cost_estimate=cost(1 << 20, 2 << 20),
        name="x_sum",
    )(own, *others)


def col_sum_kernel(matching, parts, out):
    episode = lax.axis_index("col") // (NCOL // 2)
    hot = parts[0].astype(F32)[0:8]
    for c in range(1, NCOL):
        hot += parts[c].astype(F32)[0:8]
    for q in range(NCOL):
        step = parts[matching[episode, q]].astype(F32)[8:16]
        pair = jnp.concatenate([hot, step], 0).astype(BF16)
        for x in range(NX):
            out[x, q] = pair


def col_sum(matching, parts):
    return pl.pallas_call(
        col_sum_kernel,
        out_shape=jax.ShapeDtypeStruct((NX, NCOL, 16, D), BF16),
        in_specs=[SMEM, pl.BlockSpec(memory_space=pltpu.VMEM)],
        out_specs=pl.BlockSpec(memory_space=pltpu.VMEM),
        compiler_params=params(16),
        cost_estimate=cost(1 << 20, 2 << 20),
        name="col_sum",
    )(matching, parts)


def finish_kernel(own, other, hot_table, context, hot_out, context_out):
    for from_other, parts in ((0, own), (1, other)):
        half = lax.axis_index("core") ^ from_other
        for x in range(NX):
            hot_at = pl.multiple_of(half * (HOT // 2) + x * 128, 128)
            ctx_at = pl.multiple_of(half * (CR // 2) + x * 64, 64)
            first = [parts[x, j].astype(F32) for j in range(NCOL)]
            hot = jnp.concatenate([p[0:8] for p in first], 0)
            step = jnp.concatenate([first[j][8:16] + first[j + 8][8:16] for j in range(8)], 0)
            hot_rows = hot_table[pl.ds(hot_at, 128)].astype(F32)
            hot_out[pl.ds(hot_at, 128)] = hot_rows - LEARN_RATE * hot
            ctx_rows = context[pl.ds(ctx_at, 64)].astype(F32)
            context_out[pl.ds(ctx_at, 64)] = ctx_rows - LEARN_RATE * step


def finish(own, other, hot_table, context):
    vmem = pl.BlockSpec(memory_space=pltpu.VMEM)
    return pl.pallas_call(
        finish_kernel,
        out_shape=[jax.ShapeDtypeStruct((HOT, D), F32), jax.ShapeDtypeStruct((CR, D), F32)],
        in_specs=[vmem, vmem, vmem, vmem],
        out_specs=[vmem, vmem],
        compiler_params=params(24),
        cost_estimate=cost(1 << 20, 7 << 20),
        name="finish",
    )(own, other, hot_table, context)


def vertex_kernel(col, cold_count, cold_list, received, panel, out):
    total = jnp.zeros((VS, D), F32)
    for c in range(NCOL):
        ids = live_ids(cold_list[0, c, pl.ds(col[0], 1), :], cold_count[0, c, col[0]])
        total += dot(one_hot(VS, ids), received[c], NN)
    out[...] = panel[...].astype(F32) - LEARN_RATE * total


def vertex_rows(col, cold_count, cold_list, received, panel):
    keep = lambda *shape: pl.BlockSpec(shape, lambda i, c: (0,) * len(shape))
    return pl.pallas_call(
        vertex_kernel,
        out_shape=jax.ShapeDtypeStruct((VS, D), F32),
        grid_spec=pltpu.PrefetchScalarGridSpec(
            num_scalar_prefetch=1,
            grid=(1,),
            in_specs=[
                SMEM,
                keep(1, NCOL, NCOL, CAP),
                keep(NCOL, CAP, D),
                pl.BlockSpec((VS, D), lambda i, c: (c[0], 0)),
            ],
            out_specs=keep(VS, D),
        ),
        compiler_params=params(56),
        cost_estimate=cost(1 << 28, 2 << 20),
        name="vertex_rows",
    )(col, cold_count, cold_list, received, panel)


def all_to_all(x, axes):
    return lax.all_to_all(x, axes, 0, 0, tiled=True)


def body(
    vertex_panel,
    context_panel,
    hot_table,
    matching,
    hot_map,
    cold_list,
    cold_count,
    src_code,
    ctx_rows,
    neg_tiles,
):
    col = lax.axis_index("col").astype(jnp.int32)[None]
    swap = [(0, 1), (1, 0)]

    pieces = all_to_all(context_panel.reshape(NCOL, CR // NCOL, D), "col")
    low = first_counts(src_code, ctx_rows)
    low, pieces = lax.optimization_barrier((low, pieces))
    ctx = all_to_all(pick_pieces(matching, pieces), "col")
    counts = (low, *second_counts(neg_tiles, src_code, ctx_rows))

    cold, keep, send = gradients(
        neg_tiles, cold_count, src_code, ctx_rows, vertex_panel, hot_table, hot_map[0],
        cold_list, ctx, counts,
    )
    received = all_to_all(cold, "col")
    arrived = lax.ppermute(send, "core", swap)
    parts = keep + arrived.astype(F32)
    others = [
        lax.ppermute(parts[k].astype(BF16), "x", [(i, i ^ k) for i in range(NX)])
        for k in range(1, NX)
    ]
    parts = x_sum(parts[0], others)
    received, parts = lax.optimization_barrier((received, parts))
    parts = all_to_all(parts, "col")
    parts = col_sum(matching, parts).reshape(NX * NCOL, 16, D)
    own = all_to_all(parts, ("x", "col")).reshape(NX, NCOL, 16, D)
    other = lax.ppermute(own, "core", swap)
    vertex_new = vertex_rows(col, cold_count, cold_list, received, vertex_panel)
    hot_new, context_new = finish(own, other, hot_table, context_panel)
    return (vertex_new, context_new, hot_new)


def solution(mesh):
    split_mesh = Mesh(mesh.devices.reshape(NX, NCORE, NCOL), ("x", "core", "col"))
    row = ("x", "core")
    in_specs = (
        P(row, None),
        P("col", None),
        P(),
        P(),
        P(row, "col", None),
        P(row, None, None, None),
        P(row, None, None),
        P(row, "col", None, None, None),
        P(row, "col", None, None, None),
        P(row, "col", None, None),
    )
    out_specs = (P(("x", "core", "col"), None), P("col", None), P())
    return jax.shard_map(
        body, mesh=split_mesh, in_specs=in_specs, out_specs=out_specs, check_vma=False
    )
```

```python
import functools

import jax
import jax.numpy as jnp
import numpy as np
from jax import lax
from jax.experimental import pallas as pl
from jax.experimental.pallas import tpu as pltpu
from jax.sharding import Mesh, PartitionSpec as P

NEG_WEIGHT = 0.0625
LEARN_RATE = 0.25

D = 512
BLOCK = 128
HOT = 1024
LHOT = 256
CAP = 64
VS = 256
CR = 512
NX = 4
NCORE = 2
NCOL = 16
NBLK = 128
SLOTS = LHOT + NCOL * CAP
HALF_SLOTS = SLOTS // 2
CHUNK = 16
STEPS = NBLK // CHUNK
BASE = 4096.0

F32 = jnp.float32
BF16 = jnp.bfloat16
I16 = jnp.int16
F8 = jnp.float8_e5m2
NN = (((1,), (0,)), ((), ()))
NT = (((1,), (1,)), ((), ()))
TN = (((0,), (0,)), ((), ()))


def dot(a, b, dims):
    return lax.dot_general(a, b, dims, preferred_element_type=F32)


def params(mib):
    return pltpu.CompilerParams(vmem_limit_bytes=mib * 2**20)


def cost(flops, nbytes):
    return pl.CostEstimate(flops=flops, bytes_accessed=nbytes, transcendentals=0)


def one_hot(rows, ids, weight=None):
    shape = (rows, ids.shape[1])
    index = lax.broadcasted_iota(jnp.int32, shape, 0).astype(I16)
    hit = index == jnp.broadcast_to(ids.astype(I16), shape)
    value = jnp.ones((), BF16) if weight is None else jnp.broadcast_to(weight, shape)
    return jnp.where(hit, value, jnp.zeros((), BF16))


def split(x):
    high = x.astype(BF16)
    return high, (x - high.astype(F32)).astype(BF16)


def count_step(first_row, pairs, codes, rows, left, right):
    width = right.shape[0]
    for n in range(CHUNK):
        at = slice(n * BLOCK, (n + 1) * BLOCK)
        code = codes[n : n + 1, :]
        upper = code >= HALF_SLOTS
        weight = jnp.where(upper, BASE, 1.0).astype(BF16)
        left[:, at] = one_hot(HALF_SLOTS, jnp.where(upper, code - HALF_SLOTS, code), weight)
        right[:, at] = one_hot(width, rows[n : n + 1, :] - first_row)
    packed = dot(left[...], right[...], NT)
    high = jnp.floor(packed * (1.0 / BASE))
    pairs[0:HALF_SLOTS] += packed - high * BASE
    pairs[HALF_SLOTS:SLOTS] += high


def tile_step(episode, step, tiles, tile_counts, codes, left, right):
    for n in range(CHUNK):
        at = slice(n * BLOCK, (n + 1) * BLOCK)
        code = codes[n : n + 1, :]
        tile = tiles[0, 0, episode, step * CHUNK + n]
        left[:, at] = one_hot(64, code >> 5).astype(F8)
        right[:, at] = one_hot(128, (code & 31) * 4 + tile).astype(F8)
    tile_counts[...] += dot(left[...], right[...], NT)


def first_count_kernel(codes, rows, pairs, left, right):
    @pl.when(pl.program_id(0) == 0)
    def _():
        pairs[...] = jnp.zeros_like(pairs)

    count_step(0, pairs, codes, rows, left, right)


def second_count_kernel(
    tiles, codes0, rows0, codes1, rows1, pairs0, pairs1,
    left0, right0, left1, right1, left2, right2,
):
    step = pl.program_id(0)

    @pl.when(step == 0)
    def _():
        pairs0[...] = jnp.zeros_like(pairs0)
        pairs1[...] = jnp.zeros_like(pairs1)

    count_step(CR // 2, pairs0, codes0, rows0, left0, right0)
    count_step(0, pairs1, codes1, rows1, left1, right1)
    tile_step(0, step, tiles, pairs0.at[SLOTS : SLOTS + 64, 0:128], codes0, left2, right2)


def count_scratch():
    edges = CHUNK * BLOCK
    return [pltpu.VMEM((HALF_SLOTS, edges), BF16), pltpu.VMEM((CR // 2, edges), BF16)]


def tile_scratch():
    edges = CHUNK * BLOCK
    return [pltpu.VMEM((64, edges), F8), pltpu.VMEM((128, edges), F8)]


SMEM = pl.BlockSpec(memory_space=pltpu.SMEM)


def whole(*shape):
    return pl.BlockSpec(shape, lambda i: (0,) * len(shape))


def edge_block(episode):
    return pl.BlockSpec(
        (None, None, None, CHUNK, BLOCK),
        lambda i: (0, 0, episode, jnp.minimum(i, STEPS - 1), 0),
    )


def first_counts(src_code, ctx_rows):
    return pl.pallas_call(
        first_count_kernel,
        out_shape=jax.ShapeDtypeStruct((SLOTS, CR // 2), F32),
        grid=(STEPS,),
        in_specs=[edge_block(0), edge_block(0)],
        out_specs=whole(SLOTS, CR // 2),
        scratch_shapes=count_scratch(),
        compiler_params=params(56),
        cost_estimate=cost(NBLK * BLOCK * HALF_SLOTS * CR, 3 << 20),
        name="first_counts",
    )(src_code, ctx_rows)


def second_counts(neg_tiles, src_code, ctx_rows):
    shapes = [(SLOTS + 64, CR // 2), (SLOTS, CR // 2)]
    return pl.pallas_call(
        second_count_kernel,
        out_shape=[jax.ShapeDtypeStruct(shape, F32) for shape in shapes],
        grid=(STEPS,),
        in_specs=[SMEM, edge_block(0), edge_block(0), edge_block(1), edge_block(1)],
        out_specs=[whole(*shape) for shape in shapes],
        scratch_shapes=count_scratch() + count_scratch() + tile_scratch(),
        compiler_params=params(56),
        cost_estimate=cost(2 * NBLK * BLOCK * HALF_SLOTS * CR, 6 << 20),
        name="second_counts",
    )(neg_tiles, src_code, ctx_rows, src_code, ctx_rows)


def live_ids(ids, count):
    lane = lax.broadcasted_iota(jnp.int32, ids.shape, 1)
    return jnp.where(lane < count, ids, -1)


def pick_kernel(matching, pieces, out):
    for episode in range(2):
        for reader in range(NCOL):
            partner = matching[episode, reader]
            out[reader, episode] = pieces[partner]


def pick_pieces(matching, pieces):
    rows = pieces.shape[1]
    return pl.pallas_call(
        pick_kernel,
        out_shape=jax.ShapeDtypeStruct((NCOL, 2, rows, D), BF16),
        in_specs=[
            pl.BlockSpec(memory_space=pltpu.SMEM),
            pl.BlockSpec(memory_space=pltpu.VMEM),
        ],
        out_specs=pl.BlockSpec(memory_space=pltpu.VMEM),
        compiler_params=params(16),
        cost_estimate=cost(0, 2 << 20),
        name="pick_pieces",
    )(matching, pieces)


def main_kernel(
    tiles, cold_count, codes, rows, panel, hot_table, hot_list, cold_list, ctx,
    pairs0_low, pairs0_high, counts0, pairs1_low, cold, keep, send,
    left, right, left2, right2, pairs1_high, counts1, all_slots, all_grads, ctx_acc, hot_acc,
):
    step = pl.program_id(0)
    col = lax.axis_index("col")

    @pl.when(step == 0)
    def _():
        pairs1_high[...] = jnp.zeros_like(pairs1_high)
        counts1[...] = jnp.zeros_like(counts1)
        all_slots[0:LHOT] = dot(one_hot(HOT, hot_list[...]), hot_table[...], TN).astype(BF16)

    @pl.when(step < STEPS)
    def _():
        for o in range(2):
            owner = 2 * step + o
            ids = live_ids(cold_list[0, col, pl.ds(owner, 1), :], cold_count[0, col, owner])
            taken = dot(one_hot(VS, ids), panel[o * VS : (o + 1) * VS, :], TN)
            at = pl.multiple_of(LHOT + owner * CAP, CAP)
            all_slots[pl.ds(at, CAP)] = taken.astype(BF16)
        count_step(CR // 2, pairs1_high, codes, rows, left, right)
        tile_step(1, step, tiles, counts1, codes, left2, right2)

    @pl.when(step >= STEPS)
    def _():
        grad_step(
            step - STEPS, hot_list, ctx, pairs0_low, pairs0_high, counts0, pairs1_low, cold, keep,
            send, pairs1_high, counts1, all_slots, all_grads, ctx_acc, hot_acc,
        )


def grad_step(
    step, hot_list, ctx, pairs0_low, pairs0_high, counts0, pairs1_low, cold, keep, send,
    pairs1_high, counts1, all_slots, all_grads, ctx_acc, hot_acc,
):
    slot_rows = pl.ds(pl.multiple_of(step * LHOT, LHOT), LHOT)
    here = all_slots[slot_rows]
    slot_at = step * LHOT + lax.broadcasted_iota(jnp.int32, (LHOT, 64), 0)
    group = ((slot_at >> 5) == lax.broadcasted_iota(jnp.int32, (LHOT, 64), 1)).astype(F32).astype(BF16)
    lane = lax.broadcasted_iota(jnp.int32, (LHOT, 256), 1)
    slot_in = lax.broadcasted_iota(jnp.int32, (LHOT, 256), 0) & 31
    mine = ((lane & 127) >> 2) == slot_in
    pick_row = lax.broadcasted_iota(jnp.int32, (256, 128), 0)
    pick_col = lax.broadcasted_iota(jnp.int32, (256, 128), 1)
    spread = jnp.where(
        (pick_row & 3) == pick_col, jnp.where(pick_row >= 128, 128.0, 1.0), 0.0
    ).astype(BF16)
    total = None
    grads = []
    for episode in range(2):
        panel = ctx[:, episode].reshape(CR, D)
        if episode == 0:
            counted = jnp.concatenate([pairs0_low[...], pairs0_high[...]], 1)
        else:
            counted = jnp.concatenate([pairs1_low[...], pairs1_high[slot_rows]], 1)
        table = (counts0, counts1)[episode][...]
        upper = jnp.floor(table * (1.0 / 128.0))
        both = jnp.concatenate([table - upper * 128.0, upper], 1).astype(BF16)
        taken = jnp.where(mine, dot(group, both, NN), 0.0).astype(BF16)
        by_tile = dot(taken, spread, NN)
        tiled = jnp.concatenate(
            [jnp.broadcast_to(by_tile[:, t : t + 1], (LHOT, BLOCK)) for t in range(4)], 1
        )
        curve = jnp.tanh(0.5 * dot(here, panel, NT))
        negative = (0.5 * NEG_WEIGHT + (0.5 * NEG_WEIGHT) * curve).astype(BF16).astype(F32)
        grad = tiled * negative - counted * (0.5 - 0.5 * curve)
        high = grad.astype(BF16)
        grads.append((grad, high, panel))
        part = dot(high, panel, NN)
        total = part if total is None else total + part
        all_grads[episode, slot_rows] = high

    @pl.when(step == 0)
    def _():
        full = total
        for grad, high, panel in grads:
            full = full + dot((grad - high.astype(F32)).astype(BF16), panel, NN)
        upper, lower = split(full)
        where_hot = one_hot(HOT, hot_list[...])
        hot_acc[...] = dot(where_hot, upper, NN) + dot(where_hot, lower, NN)

    @pl.when(step > 0)
    def _():
        for o in range(4):
            cold[o] = total[o * CAP : (o + 1) * CAP].astype(BF16)

    @pl.when(step == 4)
    def _():
        for episode in range(2):
            ctx_acc[episode] = dot(all_grads[episode], all_slots[...], TN)
        core = lax.axis_index("core")
        for half, out in ((core, keep), (1 - core, send)):
            for away in range(NX):
                x = lax.axis_index("x") ^ away
                hot_at = pl.multiple_of(half * (HOT // 2) + x * 128, 128)
                ctx_at = pl.multiple_of(half * (CR // 2) + x * 64, 64)
                out[away, 0:128] = hot_acc[pl.ds(hot_at, 128)].astype(out.dtype)
                out[away, 128:192] = ctx_acc[0, pl.ds(ctx_at, 64)].astype(out.dtype)
                out[away, 192:256] = ctx_acc[1, pl.ds(ctx_at, 64)].astype(out.dtype)


def gradients(
    neg_tiles, cold_count, src_code, ctx_rows, panel, hot_table, hot_list, cold_list, ctx, counts
):
    later = lambda i: jnp.maximum(i - STEPS, 0)
    half = pl.BlockSpec((LHOT, CR // 2), lambda i: (later(i), 0))
    part = lambda dtype: jax.ShapeDtypeStruct((NX, 256, D), dtype)
    return pl.pallas_call(
        main_kernel,
        out_shape=[jax.ShapeDtypeStruct((NCOL, CAP, D), BF16), part(F32), part(BF16)],
        grid=(STEPS + 5,),
        in_specs=[
            SMEM,
            SMEM,
            edge_block(1),
            edge_block(1),
            pl.BlockSpec((2 * VS, D), lambda i: (jnp.minimum(i, STEPS - 1), 0)),
            whole(HOT, D),
            whole(1, LHOT),
            whole(1, NCOL, NCOL, CAP),
            whole(NCOL, 2, CR // NCOL, D),
            half,
            half,
            pl.BlockSpec((64, 128), lambda i: (SLOTS // 64, 0)),
            half,
        ],
        out_specs=[
            pl.BlockSpec((4, CAP, D), lambda i: (later(i - 1), 0, 0)),
            whole(NX, 256, D),
            whole(NX, 256, D),
        ],
        scratch_shapes=count_scratch()
        + tile_scratch()
        + [
            pltpu.VMEM((SLOTS, CR // 2), F32),
            pltpu.VMEM((64, 128), F32),
            pltpu.VMEM((SLOTS, D), BF16),
            pltpu.VMEM((2, SLOTS, CR), BF16),
            pltpu.VMEM((2, CR, D), F32),
            pltpu.VMEM((HOT, D), F32),
        ],
        compiler_params=params(50),
        cost_estimate=cost(28 << 30, 12 << 20),
        name="gradients",
    )(
        neg_tiles, cold_count, src_code, ctx_rows, panel, hot_table, hot_list, cold_list, ctx,
        *counts,
    )


def x_sum_kernel(own, first, second, third, out):
    total = own[...]
    for part in (first, second, third):
        total += part[...].astype(F32)
    for j in range(NCOL):
        pair = jnp.concatenate([total[j * 8 : j * 8 + 8], total[128 + j * 8 : 136 + j * 8]], 0)
        out[j] = pair.astype(BF16)


def x_sum(own, others):
    return pl.pallas_call(
        x_sum_kernel,
        out_shape=jax.ShapeDtypeStruct((NCOL, 16, D), BF16),
        compiler_params=params(16),
        cost_estimate=cost(1 << 20, 2 << 20),
        name="x_sum",
    )(own, *others)


def col_sum_kernel(matching, parts, out):
    episode = lax.axis_index("col") // (NCOL // 2)
    hot = parts[0].astype(F32)[0:8]
    for c in range(1, NCOL):
        hot += parts[c].astype(F32)[0:8]
    for q in range(NCOL):
        step = parts[matching[episode, q]].astype(F32)[8:16]
        pair = jnp.concatenate([hot, step], 0).astype(BF16)
        for x in range(NX):
            out[x, q] = pair


def col_sum(matching, parts):
    return pl.pallas_call(
        col_sum_kernel,
        out_shape=jax.ShapeDtypeStruct((NX, NCOL, 16, D), BF16),
        in_specs=[SMEM, pl.BlockSpec(memory_space=pltpu.VMEM)],
        out_specs=pl.BlockSpec(memory_space=pltpu.VMEM),
        compiler_params=params(16),
        cost_estimate=cost(1 << 20, 2 << 20),
        name="col_sum",
    )(matching, parts)


def finish_kernel(own, other, hot_table, context, hot_out, context_out):
    for from_other, parts in ((0, own), (1, other)):
        half = lax.axis_index("core") ^ from_other
        for x in range(NX):
            hot_at = pl.multiple_of(half * (HOT // 2) + x * 128, 128)
            ctx_at = pl.multiple_of(half * (CR // 2) + x * 64, 64)
            first = [parts[x, j].astype(F32) for j in range(NCOL)]
            hot = jnp.concatenate([p[0:8] for p in first], 0)
            step = jnp.concatenate([first[j][8:16] + first[j + 8][8:16] for j in range(8)], 0)
            hot_rows = hot_table[pl.ds(hot_at, 128)].astype(F32)
            hot_out[pl.ds(hot_at, 128)] = hot_rows - LEARN_RATE * hot
            ctx_rows = context[pl.ds(ctx_at, 64)].astype(F32)
            context_out[pl.ds(ctx_at, 64)] = ctx_rows - LEARN_RATE * step


def finish(own, other, hot_table, context):
    vmem = pl.BlockSpec(memory_space=pltpu.VMEM)
    return pl.pallas_call(
        finish_kernel,
        out_shape=[jax.ShapeDtypeStruct((HOT, D), F32), jax.ShapeDtypeStruct((CR, D), F32)],
        in_specs=[vmem, vmem, vmem, vmem],
        out_specs=[vmem, vmem],
        compiler_params=params(24),
        cost_estimate=cost(1 << 20, 7 << 20),
        name="finish",
    )(own, other, hot_table, context)


def vertex_kernel(col, cold_count, cold_list, received, panel, out):
    total = jnp.zeros((VS, D), F32)
    for c in range(NCOL):
        ids = live_ids(cold_list[0, c, pl.ds(col[0], 1), :], cold_count[0, c, col[0]])
        total += dot(one_hot(VS, ids), received[c], NN)
    out[...] = panel[...].astype(F32) - LEARN_RATE * total


def vertex_rows(col, cold_count, cold_list, received, panel):
    keep = lambda *shape: pl.BlockSpec(shape, lambda i, c: (0,) * len(shape))
    return pl.pallas_call(
        vertex_kernel,
        out_shape=jax.ShapeDtypeStruct((VS, D), F32),
        grid_spec=pltpu.PrefetchScalarGridSpec(
            num_scalar_prefetch=1,
            grid=(1,),
            in_specs=[
                SMEM,
                keep(1, NCOL, NCOL, CAP),
                keep(NCOL, CAP, D),
                pl.BlockSpec((VS, D), lambda i, c: (c[0], 0)),
            ],
            out_specs=keep(VS, D),
        ),
        compiler_params=params(56),
        cost_estimate=cost(1 << 28, 2 << 20),
        name="vertex_rows",
    )(col, cold_count, cold_list, received, panel)


def all_to_all(x, axes):
    return lax.all_to_all(x, axes, 0, 0, tiled=True)


def body(
    vertex_panel,
    context_panel,
    hot_table,
    matching,
    hot_map,
    cold_list,
    cold_count,
    src_code,
    ctx_rows,
    neg_tiles,
):
    col = lax.axis_index("col").astype(jnp.int32)[None]
    swap = [(0, 1), (1, 0)]

    pieces = all_to_all(context_panel.reshape(NCOL, CR // NCOL, D), "col")
    low = first_counts(src_code, ctx_rows)
    low, pieces = lax.optimization_barrier((low, pieces))
    ctx = all_to_all(pick_pieces(matching, pieces), "col")
    high, second = second_counts(neg_tiles, src_code, ctx_rows)
    counts = (low, high, high, second)

    cold, keep, send = gradients(
        neg_tiles, cold_count, src_code, ctx_rows, vertex_panel, hot_table, hot_map[0],
        cold_list, ctx, counts,
    )
    received = all_to_all(cold, "col")
    arrived = lax.ppermute(send, "core", swap)
    parts = keep + arrived.astype(F32)
    others = [
        lax.ppermute(parts[k].astype(BF16), "x", [(i, i ^ k) for i in range(NX)])
        for k in range(1, NX)
    ]
    parts = x_sum(parts[0], others)
    received, parts = lax.optimization_barrier((received, parts))
    parts = all_to_all(parts, "col")
    parts = col_sum(matching, parts).reshape(NX * NCOL, 16, D)
    own = all_to_all(parts, ("x", "col")).reshape(NX, NCOL, 16, D)
    other = lax.ppermute(own, "core", swap)
    vertex_new = vertex_rows(col, cold_count, cold_list, received, vertex_panel)
    hot_new, context_new = finish(own, other, hot_table, context_panel)
    return (vertex_new, context_new, hot_new)


def solution(mesh):
    split_mesh = Mesh(mesh.devices.reshape(NX, NCORE, NCOL), ("x", "core", "col"))
    row = ("x", "core")
    in_specs = (
        P(row, None),
        P("col", None),
        P(),
        P(),
        P(row, "col", None),
        P(row, None, None, None),
        P(row, None, None),
        P(row, "col", None, None, None),
        P(row, "col", None, None, None),
        P(row, "col", None, None),
    )
    out_specs = (P(("x", "core", "col"), None), P("col", None), P())
    return jax.shard_map(
        body, mesh=split_mesh, in_specs=in_specs, out_specs=out_specs, check_vma=False
    )
```

```python
import functools

import jax
import jax.numpy as jnp
import numpy as np
from jax import lax
from jax.experimental import pallas as pl
from jax.experimental.pallas import tpu as pltpu
from jax.sharding import Mesh, PartitionSpec as P

NEG_WEIGHT = 0.0625
LEARN_RATE = 0.25

D = 512
BLOCK = 128
HOT = 1024
LHOT = 256
CAP = 64
VS = 256
CR = 512
NX = 4
NCORE = 2
NCOL = 16
NBLK = 128
SLOTS = LHOT + NCOL * CAP
HALF_SLOTS = SLOTS // 2
CHUNK = 16
STEPS = NBLK // CHUNK
BASE = 4096.0

F32 = jnp.float32
BF16 = jnp.bfloat16
I16 = jnp.int16
F8 = jnp.float8_e5m2
NN = (((1,), (0,)), ((), ()))
NT = (((1,), (1,)), ((), ()))
TN = (((0,), (0,)), ((), ()))


def dot(a, b, dims):
    return lax.dot_general(a, b, dims, preferred_element_type=F32)


def params(mib):
    return pltpu.CompilerParams(vmem_limit_bytes=mib * 2**20)


def cost(flops, nbytes):
    return pl.CostEstimate(flops=flops, bytes_accessed=nbytes, transcendentals=0)


def one_hot(rows, ids, weight=None):
    shape = (rows, ids.shape[1])
    index = lax.broadcasted_iota(jnp.int32, shape, 0).astype(I16)
    hit = index == jnp.broadcast_to(ids.astype(I16), shape)
    value = jnp.ones((), BF16) if weight is None else jnp.broadcast_to(weight, shape)
    return jnp.where(hit, value, jnp.zeros((), BF16))


def split(x):
    high = x.astype(BF16)
    return high, (x - high.astype(F32)).astype(BF16)


def count_step(first_row, pairs, codes, rows, left, right):
    width = right.shape[0]
    for n in range(CHUNK):
        at = slice(n * BLOCK, (n + 1) * BLOCK)
        code = codes[n : n + 1, :]
        upper = code >= HALF_SLOTS
        weight = jnp.where(upper, BASE, 1.0).astype(BF16)
        left[:, at] = one_hot(HALF_SLOTS, jnp.where(upper, code - HALF_SLOTS, code), weight)
        right[:, at] = one_hot(width, rows[n : n + 1, :] - first_row)
    packed = dot(left[...], right[...], NT)
    high = jnp.floor(packed * (1.0 / BASE))
    pairs[0:HALF_SLOTS] += packed - high * BASE
    pairs[HALF_SLOTS:SLOTS] += high


def tile_step(episode, step, tiles, tile_counts, codes, left, right):
    for n in range(CHUNK):
        at = slice(n * BLOCK, (n + 1) * BLOCK)
        code = codes[n : n + 1, :]
        tile = tiles[0, 0, episode, step * CHUNK + n]
        left[:, at] = one_hot(64, code >> 5).astype(F8)
        right[:, at] = one_hot(128, (code & 31) * 4 + tile).astype(F8)
    tile_counts[...] += dot(left[...], right[...], NT)


def first_count_kernel(codes, rows, pairs, left, right):
    @pl.when(pl.program_id(0) == 0)
    def _():
        pairs[...] = jnp.zeros_like(pairs)

    count_step(0, pairs, codes, rows, left, right)


def second_count_kernel(
    tiles, codes0, rows0, codes1, rows1, pairs0, pairs1,
    left0, right0, left1, right1, left2, right2,
):
    step = pl.program_id(0)

    @pl.when(step == 0)
    def _():
        pairs0[...] = jnp.zeros_like(pairs0)
        pairs1[...] = jnp.zeros_like(pairs1)

    count_step(CR // 2, pairs0, codes0, rows0, left0, right0)
    count_step(0, pairs1, codes1, rows1, left1, right1)
    tile_step(0, step, tiles, pairs0.at[SLOTS : SLOTS + 64, 0:128], codes0, left2, right2)


def count_scratch():
    edges = CHUNK * BLOCK
    return [pltpu.VMEM((HALF_SLOTS, edges), BF16), pltpu.VMEM((CR // 2, edges), BF16)]


def tile_scratch():
    edges = CHUNK * BLOCK
    return [pltpu.VMEM((64, edges), F8), pltpu.VMEM((128, edges), F8)]


SMEM = pl.BlockSpec(memory_space=pltpu.SMEM)


def whole(*shape):
    return pl.BlockSpec(shape, lambda i: (0,) * len(shape))


def edge_block(episode):
    return pl.BlockSpec(
        (None, None, None, CHUNK, BLOCK),
        lambda i: (0, 0, episode, jnp.minimum(i, STEPS - 1), 0),
    )


def first_counts(src_code, ctx_rows):
    return pl.pallas_call(
        first_count_kernel,
        out_shape=jax.ShapeDtypeStruct((SLOTS, CR // 2), F32),
        grid=(STEPS,),
        in_specs=[edge_block(0), edge_block(0)],
        out_specs=whole(SLOTS, CR // 2),
        scratch_shapes=count_scratch(),
        compiler_params=params(56),
        cost_estimate=cost(NBLK * BLOCK * HALF_SLOTS * CR, 3 << 20),
        name="first_counts",
    )(src_code, ctx_rows)


def second_counts(neg_tiles, src_code, ctx_rows):
    shapes = [(SLOTS + 64, CR // 2), (SLOTS, CR // 2)]
    return pl.pallas_call(
        second_count_kernel,
        out_shape=[jax.ShapeDtypeStruct(shape, F32) for shape in shapes],
        grid=(STEPS,),
        in_specs=[SMEM, edge_block(0), edge_block(0), edge_block(1), edge_block(1)],
        out_specs=[whole(*shape) for shape in shapes],
        scratch_shapes=count_scratch() + count_scratch() + tile_scratch(),
        compiler_params=params(56),
        cost_estimate=cost(2 * NBLK * BLOCK * HALF_SLOTS * CR, 6 << 20),
        name="second_counts",
    )(neg_tiles, src_code, ctx_rows, src_code, ctx_rows)


def live_ids(ids, count):
    lane = lax.broadcasted_iota(jnp.int32, ids.shape, 1)
    return jnp.where(lane < count, ids, -1)


def pick_kernel(matching, pieces, out):
    for episode in range(2):
        for reader in range(NCOL):
            partner = matching[episode, reader]
            out[reader, episode] = pieces[partner]


def pick_pieces(matching, pieces):
    rows = pieces.shape[1]
    return pl.pallas_call(
        pick_kernel,
        out_shape=jax.ShapeDtypeStruct((NCOL, 2, rows, D), BF16),
        in_specs=[
            pl.BlockSpec(memory_space=pltpu.SMEM),
            pl.BlockSpec(memory_space=pltpu.VMEM),
        ],
        out_specs=pl.BlockSpec(memory_space=pltpu.VMEM),
        compiler_params=params(16),
        cost_estimate=cost(0, 2 << 20),
        name="pick_pieces",
    )(matching, pieces)


def main_kernel(
    tiles, cold_count, codes, rows, panel, hot_table, hot_list, cold_list, ctx,
    pairs0_low, pairs0_high, counts0, pairs1_low, cold, keep, send,
    left, right, left2, right2, pairs1_high, counts1, all_slots, all_grads, ctx_acc, hot_acc,
):
    step = pl.program_id(0)
    col = lax.axis_index("col")

    @pl.when(step == 0)
    def _():
        pairs1_high[...] = jnp.zeros_like(pairs1_high)
        counts1[...] = jnp.zeros_like(counts1)
        all_slots[0:LHOT] = dot(one_hot(HOT, hot_list[...]), hot_table[...], TN).astype(BF16)

    @pl.when(step < STEPS)
    def _():
        for o in range(2):
            owner = 2 * step + o
            ids = live_ids(cold_list[0, col, pl.ds(owner, 1), :], cold_count[0, col, owner])
            taken = dot(one_hot(VS, ids), panel[o * VS : (o + 1) * VS, :], TN)
            at = pl.multiple_of(LHOT + owner * CAP, CAP)
            all_slots[pl.ds(at, CAP)] = taken.astype(BF16)
        count_step(CR // 2, pairs1_high, codes, rows, left, right)
        tile_step(1, step, tiles, counts1, codes, left2, right2)

    @pl.when(step >= STEPS)
    def _():
        grad_step(
            step - STEPS, hot_list, ctx, pairs0_low, pairs0_high, counts0, pairs1_low, cold, keep,
            send, pairs1_high, counts1, all_slots, all_grads, ctx_acc, hot_acc,
        )


def grad_step(
    step, hot_list, ctx, pairs0_low, pairs0_high, counts0, pairs1_low, cold, keep, send,
    pairs1_high, counts1, all_slots, all_grads, ctx_acc, hot_acc,
):
    slot_rows = pl.ds(pl.multiple_of(step * LHOT, LHOT), LHOT)
    here = all_slots[slot_rows]
    slot_at = step * LHOT + lax.broadcasted_iota(jnp.int32, (LHOT, 64), 0)
    group = ((slot_at >> 5) == lax.broadcasted_iota(jnp.int32, (LHOT, 64), 1)).astype(F32).astype(BF16)
    lane = lax.broadcasted_iota(jnp.int32, (LHOT, 256), 1)
    slot_in = lax.broadcasted_iota(jnp.int32, (LHOT, 256), 0) & 31
    mine = ((lane & 127) >> 2) == slot_in
    pick_row = lax.broadcasted_iota(jnp.int32, (256, 128), 0)
    pick_col = lax.broadcasted_iota(jnp.int32, (256, 128), 1)
    spread = jnp.where(
        (pick_row & 3) == pick_col, jnp.where(pick_row >= 128, 128.0, 1.0), 0.0
    ).astype(BF16)
    total = None
    grads = []
    for episode in range(2):
        panel = ctx[:, episode].reshape(CR, D)
        if episode == 0:
            counted = jnp.concatenate([pairs0_low[...], pairs0_high[...]], 1)
        else:
            counted = jnp.concatenate([pairs1_low[...], pairs1_high[slot_rows]], 1)
        table = (counts0, counts1)[episode][...]
        upper = jnp.floor(table * (1.0 / 128.0))
        both = jnp.concatenate([table - upper * 128.0, upper], 1).astype(BF16)
        taken = jnp.where(mine, dot(group, both, NN), 0.0).astype(BF16)
        by_tile = dot(taken, spread, NN)
        tiled = jnp.concatenate(
            [jnp.broadcast_to(by_tile[:, t : t + 1], (LHOT, BLOCK)) for t in range(4)], 1
        )
        curve = jnp.tanh(0.5 * dot(here, panel, NT))
        negative = (0.5 * NEG_WEIGHT + (0.5 * NEG_WEIGHT) * curve).astype(BF16).astype(F32)
        grad = tiled * negative - counted * (0.5 - 0.5 * curve)
        high = grad.astype(BF16)
        grads.append((grad, high, panel))
        part = dot(high, panel, NN)
        total = part if total is None else total + part
        all_grads[episode, slot_rows] = high

    @pl.when(step == 0)
    def _():
        full = total
        for grad, high, panel in grads:
            full = full + dot((grad - high.astype(F32)).astype(BF16), panel, NN)
        upper, lower = split(full)
        where_hot = one_hot(HOT, hot_list[...])
        hot_acc[...] = dot(where_hot, upper, NN) + dot(where_hot, lower, NN)

    @pl.when(step > 0)
    def _():
        for o in range(4):
            cold[o] = total[o * CAP : (o + 1) * CAP].astype(BF16)

    @pl.when(step == 4)
    def _():
        for episode in range(2):
            ctx_acc[episode] = dot(all_grads[episode], all_slots[...], TN)
        core = lax.axis_index("core")
        for half, out in ((core, keep), (1 - core, send)):
            for away in range(NX):
                x = lax.axis_index("x") ^ away
                hot_at = pl.multiple_of(half * (HOT // 2) + x * 128, 128)
                ctx_at = pl.multiple_of(half * (CR // 2) + x * 64, 64)
                out[away, 0:128] = hot_acc[pl.ds(hot_at, 128)].astype(out.dtype)
                out[away, 128:192] = ctx_acc[0, pl.ds(ctx_at, 64)].astype(out.dtype)
                out[away, 192:256] = ctx_acc[1, pl.ds(ctx_at, 64)].astype(out.dtype)


def gradients(
    neg_tiles, cold_count, src_code, ctx_rows, panel, hot_table, hot_list, cold_list, ctx, counts
):
    later = lambda i: jnp.maximum(i - STEPS, 0)
    half = pl.BlockSpec((LHOT, CR // 2), lambda i: (later(i), 0))
    part = lambda dtype: jax.ShapeDtypeStruct((NX, 256, D), dtype)
    return pl.pallas_call(
        main_kernel,
        out_shape=[jax.ShapeDtypeStruct((NCOL, CAP, D), BF16), part(F32), part(BF16)],
        grid=(STEPS + 5,),
        in_specs=[
            SMEM,
            SMEM,
            edge_block(1),
            edge_block(1),
            pl.BlockSpec((2 * VS, D), lambda i: (jnp.minimum(i, STEPS - 1), 0)),
            whole(HOT, D),
            whole(1, LHOT),
            whole(1, NCOL, NCOL, CAP),
            whole(NCOL, 2, CR // NCOL, D),
            half,
            half,
            pl.BlockSpec((64, 128), lambda i: (SLOTS // 64, 0)),
            half,
        ],
        out_specs=[
            pl.BlockSpec((4, CAP, D), lambda i: (later(i - 1), 0, 0)),
            whole(NX, 256, D),
            whole(NX, 256, D),
        ],
        scratch_shapes=count_scratch()
        + tile_scratch()
        + [
            pltpu.VMEM((SLOTS, CR // 2), F32),
            pltpu.VMEM((64, 128), F32),
            pltpu.VMEM((SLOTS, D), BF16),
            pltpu.VMEM((2, SLOTS, CR), BF16),
            pltpu.VMEM((2, CR, D), F32),
            pltpu.VMEM((HOT, D), F32),
        ],
        compiler_params=params(49),
        cost_estimate=cost(28 << 30, 12 << 20),
        name="gradients",
    )(
        neg_tiles, cold_count, src_code, ctx_rows, panel, hot_table, hot_list, cold_list, ctx,
        *counts,
    )


def x_sum_kernel(own, first, second, third, out):
    total = own[...]
    for part in (first, second, third):
        total += part[...].astype(F32)
    for j in range(NCOL):
        pair = jnp.concatenate([total[j * 8 : j * 8 + 8], total[128 + j * 8 : 136 + j * 8]], 0)
        out[j] = pair.astype(BF16)


def x_sum(own, others):
    return pl.pallas_call(
        x_sum_kernel,
        out_shape=jax.ShapeDtypeStruct((NCOL, 16, D), BF16),
        compiler_params=params(16),
        cost_estimate=cost(1 << 20, 2 << 20),
        name="x_sum",
    )(own, *others)


def col_sum_kernel(matching, parts, out):
    episode = lax.axis_index("col") // (NCOL // 2)
    hot = parts[0].astype(F32)[0:8]
    for c in range(1, NCOL):
        hot += parts[c].astype(F32)[0:8]
    for q in range(NCOL):
        step = parts[matching[episode, q]].astype(F32)[8:16]
        pair = jnp.concatenate([hot, step], 0).astype(BF16)
        for x in range(NX):
            out[x, q] = pair


def col_sum(matching, parts):
    return pl.pallas_call(
        col_sum_kernel,
        out_shape=jax.ShapeDtypeStruct((NX, NCOL, 16, D), BF16),
        in_specs=[SMEM, pl.BlockSpec(memory_space=pltpu.VMEM)],
        out_specs=pl.BlockSpec(memory_space=pltpu.VMEM),
        compiler_params=params(16),
        cost_estimate=cost(1 << 20, 2 << 20),
        name="col_sum",
    )(matching, parts)


def finish_kernel(own, other, hot_table, context, hot_out, context_out):
    for from_other, parts in ((0, own), (1, other)):
        half = lax.axis_index("core") ^ from_other
        for x in range(NX):
            hot_at = pl.multiple_of(half * (HOT // 2) + x * 128, 128)
            ctx_at = pl.multiple_of(half * (CR // 2) + x * 64, 64)
            first = [parts[x, j].astype(F32) for j in range(NCOL)]
            hot = jnp.concatenate([p[0:8] for p in first], 0)
            step = jnp.concatenate([first[j][8:16] + first[j + 8][8:16] for j in range(8)], 0)
            hot_rows = hot_table[pl.ds(hot_at, 128)].astype(F32)
            hot_out[pl.ds(hot_at, 128)] = hot_rows - LEARN_RATE * hot
            ctx_rows = context[pl.ds(ctx_at, 64)].astype(F32)
            context_out[pl.ds(ctx_at, 64)] = ctx_rows - LEARN_RATE * step


def finish(own, other, hot_table, context):
    vmem = pl.BlockSpec(memory_space=pltpu.VMEM)
    return pl.pallas_call(
        finish_kernel,
        out_shape=[jax.ShapeDtypeStruct((HOT, D), F32), jax.ShapeDtypeStruct((CR, D), F32)],
        in_specs=[vmem, vmem, vmem, vmem],
        out_specs=[vmem, vmem],
        compiler_params=params(24),
        cost_estimate=cost(1 << 20, 7 << 20),
        name="finish",
    )(own, other, hot_table, context)


def vertex_kernel(col, cold_count, cold_list, received, panel, out):
    total = jnp.zeros((VS, D), F32)
    for c in range(NCOL):
        ids = live_ids(cold_list[0, c, pl.ds(col[0], 1), :], cold_count[0, c, col[0]])
        total += dot(one_hot(VS, ids), received[c], NN)
    out[...] = panel[...].astype(F32) - LEARN_RATE * total


def vertex_rows(col, cold_count, cold_list, received, panel):
    keep = lambda *shape: pl.BlockSpec(shape, lambda i, c: (0,) * len(shape))
    return pl.pallas_call(
        vertex_kernel,
        out_shape=jax.ShapeDtypeStruct((VS, D), F32),
        grid_spec=pltpu.PrefetchScalarGridSpec(
            num_scalar_prefetch=1,
            grid=(1,),
            in_specs=[
                SMEM,
                keep(1, NCOL, NCOL, CAP),
                keep(NCOL, CAP, D),
                pl.BlockSpec((VS, D), lambda i, c: (c[0], 0)),
            ],
            out_specs=keep(VS, D),
        ),
        compiler_params=params(56),
        cost_estimate=cost(1 << 28, 2 << 20),
        name="vertex_rows",
    )(col, cold_count, cold_list, received, panel)


def all_to_all(x, axes):
    return lax.all_to_all(x, axes, 0, 0, tiled=True)


def body(
    vertex_panel,
    context_panel,
    hot_table,
    matching,
    hot_map,
    cold_list,
    cold_count,
    src_code,
    ctx_rows,
    neg_tiles,
):
    col = lax.axis_index("col").astype(jnp.int32)[None]
    swap = [(0, 1), (1, 0)]

    pieces = all_to_all(context_panel.reshape(NCOL, CR // NCOL, D), "col")
    low = first_counts(src_code, ctx_rows)
    low, pieces = lax.optimization_barrier((low, pieces))
    ctx = all_to_all(pick_pieces(matching, pieces), "col")
    high, second = second_counts(neg_tiles, src_code, ctx_rows)
    counts = (low, high, high, second)

    cold, keep, send = gradients(
        neg_tiles, cold_count, src_code, ctx_rows, vertex_panel, hot_table, hot_map[0],
        cold_list, ctx, counts,
    )
    received = all_to_all(cold, "col")
    arrived = lax.ppermute(send, "core", swap)
    parts = keep + arrived.astype(F32)
    others = [
        lax.ppermute(parts[k].astype(BF16), "x", [(i, i ^ k) for i in range(NX)])
        for k in range(1, NX)
    ]
    parts = x_sum(parts[0], others)
    received, parts = lax.optimization_barrier((received, parts))
    parts = all_to_all(parts, "col")
    parts = col_sum(matching, parts).reshape(NX * NCOL, 16, D)
    own = all_to_all(parts, ("x", "col")).reshape(NX, NCOL, 16, D)
    other = lax.ppermute(own, "core", swap)
    vertex_new = vertex_rows(col, cold_count, cold_list, received, vertex_panel)
    hot_new, context_new = finish(own, other, hot_table, context_panel)
    return (vertex_new, context_new, hot_new)


def solution(mesh):
    split_mesh = Mesh(mesh.devices.reshape(NX, NCORE, NCOL), ("x", "core", "col"))
    row = ("x", "core")
    in_specs = (
        P(row, None),
        P("col", None),
        P(),
        P(),
        P(row, "col", None),
        P(row, None, None, None),
        P(row, None, None),
        P(row, "col", None, None, None),
        P(row, "col", None, None, None),
        P(row, "col", None, None),
    )
    out_specs = (P(("x", "core", "col"), None), P("col", None), P())
    return jax.shard_map(
        body, mesh=split_mesh, in_specs=in_specs, out_specs=out_specs, check_vma=False
    )
```
